1024 devices in a mesh: gz: 128 (over x, z, core), gy: 8 (over y).
Axes of the slice: x: 4, y: 8, z: 16, core: 2. Of those that a mesh axis runs over, the one named last changes fastest.
Arguments:
- velocity: float32 [3, 2048, 128, 256], P(None, 'gz', 'gy'), may hold values from -14 to 14
Outputs:
- increment: float32 [3, 2048, 128, 256], P(None, 'gz', 'gy')
The draws below stay inside these ranges and needn't reach their ends.
All inputs are finite; a program needn't handle non-finite values. Where the reference program divides by a largest or mean magnitude, that divisor is 1e-20 or more.
Results may differ from the reference program's by a relative error of at most 0.00011.
Values sent between devices are 32-bit elements; how exact they have to be, the bound alone decides.
No kernel may reach another device: no remote copies, remote signals or barrier semaphores. Data moves between devices by JAX's collectives and lax.ppermute only.
A program may use at most 64 MiB of HBM per device.

```python
import jax
import jax.numpy as jnp
from jax import lax

CZ = 16
NX = 256
NZ = 2048
NY = 128


def draw_velocity(key, part):
    phases = jax.random.uniform(jax.random.fold_in(key, 11), (2,), jnp.float32, 0.0, 1.0)
    parity = jax.random.randint(jax.random.fold_in(key, 13), (), 0, 2)
    zpos = jnp.mod(jnp.arange(NZ, dtype=jnp.float32) / NZ + phases[0], 1.0)
    ypos = jnp.mod(jnp.arange(NY, dtype=jnp.float32) / NY + phases[1], 1.0)
    slab_ids = (jnp.arange(NZ, dtype=jnp.int32) // CZ + parity) % 2
    contrast = jnp.where(slab_ids == 0, 1.0, 1.0 / 16.0).astype(jnp.float32)
    amplitude = (contrast * (1.0 + 2.0 * zpos))[:, None, None] * (1.0 + 2.0 * ypos)[None, :, None] / 3.0
    noise_key = jax.random.fold_in(key, 17)
    base = jnp.clip(jax.random.normal(noise_key, (3, NZ, NY, NX), jnp.float32), -4.5, 4.5)
    return amplitude[None] * base


def setup_inputs(seed: int = 0) -> dict:
    seeds = jax.random.split(jax.random.key(seed), 2)
    velocity = draw_velocity(jax.random.fold_in(seeds[1], 71), 0)
    return {"velocity": velocity}


FIRST_NEAR = 14.0 / 9.0
FIRST_FAR = 1.0 / 9.0
SECOND_NEAR = 12.0 / 11.0
SECOND_FAR = 3.0 / 11.0
VISCOSITY = 1.0
COURANT = 4.0
FIRST_ROOT = -0.38196601125010515
SECOND_ROOT = -0.18826230851010055


def shifted(field, offset):
    return jnp.roll(field, -offset, axis=1)


def sources_of(block):
    vertical = block[2]
    fluxes = vertical[None] * block
    first_rhs = 0.5 * FIRST_NEAR * (shifted(fluxes, 1) - shifted(fluxes, -1)) + 0.25 * FIRST_FAR * (shifted(fluxes, 2) - shifted(fluxes, -2))
    second_rhs = SECOND_NEAR * (shifted(block, 1) - 2.0 * block + shifted(block, -1)) + 0.25 * SECOND_FAR * (shifted(block, 2) - 2.0 * block + shifted(block, -2))
    return jnp.concatenate([first_rhs, second_rhs], axis=0)


def cyclic_solve(sources, factors):
    planes_first = jnp.moveaxis(sources, 1, 0)

    def advance(state, plane_row):
        updated = plane_row + factors * state
        return updated, updated

    start = jnp.zeros_like(planes_first[0])
    wrapped, _ = lax.scan(advance, start, planes_first)
    _, forward = lax.scan(advance, wrapped, planes_first)
    wrapped_back, _ = lax.scan(advance, start, forward, reverse=True)
    _, backward = lax.scan(advance, wrapped_back, forward, reverse=True)
    return jnp.moveaxis((1.0 + factors * factors) * backward, 0, 1)


def reference(velocity):
    highest = jnp.max(jnp.sum(jnp.abs(velocity), axis=0))
    step_size = COURANT / (highest + 1e-6)
    factors = jnp.array([FIRST_ROOT] * 3 + [SECOND_ROOT] * 3, dtype=jnp.float32).reshape(6, 1, 1)
    block_cols = 16

    def one_block(number, output):
        start = (number * block_cols).astype(jnp.int32)
        block = lax.dynamic_slice_in_dim(velocity, start, block_cols, axis=3)
        solved = cyclic_solve(sources_of(block), factors)
        tendency = step_size * (VISCOSITY * solved[3:] - solved[:3])
        return lax.dynamic_update_slice_in_dim(output, tendency.astype(output.dtype), start, axis=3)

    return lax.fori_loop(0, NX // block_cols, one_block, jnp.zeros_like(velocity))
```

```python
import jax
import jax.numpy as jnp
from jax import lax
from jax.experimental import pallas as pl
from jax.experimental.pallas import tpu as pltpu
from jax.sharding import PartitionSpec as P

COURANT = 4.0
FIRST_ROOT = -0.38196601125010515
SECOND_ROOT = -0.18826230851010056
FIRST_OFF, FIRST_NEAR, FIRST_FAR = 1.0 / 3.0, 7.0 / 9.0, 1.0 / 36.0
SECOND_OFF, SECOND_NEAR, SECOND_FAR = 2.0 / 11.0, 12.0 / 11.0, 3.0 / 44.0


def filter_constants():
    r = FIRST_ROOT
    gain = 1.0 / (1.0 + 2.0 * FIRST_OFF * r)
    tail = gain * (FIRST_NEAR * (r - 1.0 / r) + FIRST_FAR * (r * r - 1.0 / (r * r)))
    first = (r, -tail * r / (1.0 - r), -gain * FIRST_FAR * (r - 1.0 / r))
    r = SECOND_ROOT
    gain = 1.0 / (1.0 + 2.0 * SECOND_OFF * r)
    tail = gain * (
        SECOND_NEAR * (r + 1.0 / r)
        + SECOND_FAR * (r * r + 1.0 / (r * r))
        - 2.0 * (SECOND_NEAR + SECOND_FAR)
    )
    second = (r, -tail * r / (1.0 - r), gain * SECOND_FAR * (r - 1.0 / r))
    return first, second


(R1, A1, E1), (R2, A2, E2) = filter_constants()


def edges_kernel(vel, peak, rightward, leftward):
    planes, rows, cols = vel.shape[1:]
    total = None
    for y in range(0, rows, 8):
        for x in range(0, cols, 128):
            at = (slice(y, y + 8), slice(x, x + 128))
            w = [vel[(2, k) + at] for k in range(planes)]
            speed = [jnp.abs(w[k]) for k in range(planes)]
            for comp in range(3):
                u = w if comp == 2 else [vel[(comp, k) + at] for k in range(planes)]
                if comp < 2:
                    speed = [s + jnp.abs(v) for s, v in zip(speed, u)]
                flux = [a * b for a, b in zip(w, u)]
                for slot, field, root in ((comp, flux, R1), (3 + comp, u, R2)):
                    step = [field[k] - field[k - 1] for k in range(1, planes)]
                    up, down = step[0], step[-1]
                    for k in range(1, planes - 1):
                        up = step[k] + root * up
                        down = step[planes - 2 - k] + root * down
                    rightward[(slot,) + at] = up
                    leftward[(slot,) + at] = down
                rightward[(6 + comp,) + at] = u[planes - 1]
                leftward[(6 + comp,) + at] = u[0]
            for s in speed:
                total = s if total is None else jnp.maximum(total, s)
    peak[...] = jnp.broadcast_to(jnp.max(total, axis=0, keepdims=True), peak.shape)


def increment_kernel(vel, peaks, from_left, from_right, out):
    planes, rows, cols = vel.shape[1:]
    scale = COURANT / (jnp.max(peaks[...], keepdims=True) + 1e-06)
    gain1 = jnp.broadcast_to(A1 * scale, (8, 128))
    gain2 = jnp.broadcast_to(A2 * scale, (8, 128))
    for y in range(0, rows, 8):
        for x in range(0, cols, 128):
            at = (slice(y, y + 8), slice(x, x + 128))
            w = [vel[(2, k) + at] for k in range(planes)]
            w = [from_left[(8,) + at]] + w + [from_right[(8,) + at]]
            w1 = [gain1 * v for v in w]
            for comp in range(3):
                if comp == 2:
                    u = w
                else:
                    u = [vel[(comp, k) + at] for k in range(planes)]
                    u = [from_left[(6 + comp,) + at]] + u + [from_right[(6 + comp,) + at]]
                f1 = [a * b for a, b in zip(w1, u)]
                f2 = [gain2 * v for v in u]
                g1 = [f1[k + 1] - f1[k] for k in range(planes + 1)]
                g2 = [f2[k + 1] - f2[k] for k in range(planes + 1)]
                p1 = gain1 * from_left[(comp,) + at]
                p2 = gain2 * from_left[(3 + comp,) + at]
                forward = []
                for k in range(planes):
                    p1 = g1[k] + R1 * p1
                    p2 = g2[k] + R2 * p2
                    forward.append(p2 - p1)
                q1 = gain1 * from_right[(comp,) + at]
                q2 = gain2 * from_right[(3 + comp,) + at]
                for k in reversed(range(planes)):
                    q1 = g1[k + 1] + R1 * q1
                    q2 = g2[k + 1] + R2 * q2
                    near = (E1 / A1) * (g1[k] + g1[k + 1]) - (E2 / A2) * (g2[k] - g2[k + 1])
                    out[(comp, k) + at] = (forward[k] - (q1 + q2)) + near


def mesh_groups(shape, free):
    count = 1
    for size in shape:
        count *= size
    groups = {}
    for flat in range(count):
        rest, coords = flat, []
        for size in reversed(shape):
            coords.append(rest % size)
            rest //= size
        coords = coords[::-1]
        key = tuple(c for axis, c in enumerate(coords) if axis not in free)
        groups.setdefault(key, []).append(flat)
    return list(groups.values())


def spread(rows, axes, groups):
    return lax.all_to_all(rows, axes, 0, 0, tiled=True, axis_index_groups=groups)


def solution(mesh):
    axes = ("gz", "gy")
    slabs, lines = mesh.shape["gz"], mesh.shape["gy"]
    ring = 16
    shape = (slabs // (2 * ring), ring, 2, lines)
    across = mesh_groups(shape, (0, 2, 3))
    along = mesh_groups(shape, (1,))

    def body(velocity):
        _, planes, rows, cols = velocity.shape
        packet = jax.ShapeDtypeStruct((9, rows, cols), jnp.float32)
        n_across, n_along = len(across[0]), len(along[0])
        peak, rightward, leftward = pl.pallas_call(
            edges_kernel,
            out_shape=(jax.ShapeDtypeStruct((n_across, 128), jnp.float32), packet, packet),
            name="edges",
        )(velocity)
        from_left = lax.ppermute(rightward, "gz", [(i, (i + 1) % slabs) for i in range(slabs)])
        from_right = lax.ppermute(leftward, "gz", [(i, (i - 1) % slabs) for i in range(slabs)])
        peak = jnp.max(spread(peak, axes, across), axis=0, keepdims=True)
        peaks = spread(jnp.broadcast_to(peak, (n_along, 128)), axes, along)
        return pl.pallas_call(
            increment_kernel,
            out_shape=jax.ShapeDtypeStruct(velocity.shape, jnp.float32),
            name="increment",
        )(velocity, peaks, from_left, from_right)

    return jax.shard_map(
        body,
        mesh=mesh,
        in_specs=(P(None, "gz", "gy", None),),
        out_specs=P(None, "gz", "gy", None),
        check_vma=False,
    )
```

```python
import jax
import jax.numpy as jnp
from jax import lax
from jax.experimental import pallas as pl
from jax.experimental.pallas import tpu as pltpu
from jax.sharding import PartitionSpec as P

COURANT = 4.0
FIRST_ROOT = -0.38196601125010515
SECOND_ROOT = -0.18826230851010056
FIRST_OFF, FIRST_NEAR, FIRST_FAR = 1.0 / 3.0, 7.0 / 9.0, 1.0 / 36.0
SECOND_OFF, SECOND_NEAR, SECOND_FAR = 2.0 / 11.0, 12.0 / 11.0, 3.0 / 44.0


def filter_constants():
    r = FIRST_ROOT
    gain = 1.0 / (1.0 + 2.0 * FIRST_OFF * r)
    tail = gain * (FIRST_NEAR * (r - 1.0 / r) + FIRST_FAR * (r * r - 1.0 / (r * r)))
    first = (r, -tail * r / (1.0 - r), -gain * FIRST_FAR * (r - 1.0 / r))
    r = SECOND_ROOT
    gain = 1.0 / (1.0 + 2.0 * SECOND_OFF * r)
    tail = gain * (
        SECOND_NEAR * (r + 1.0 / r)
        + SECOND_FAR * (r * r + 1.0 / (r * r))
        - 2.0 * (SECOND_NEAR + SECOND_FAR)
    )
    second = (r, -tail * r / (1.0 - r), gain * SECOND_FAR * (r - 1.0 / r))
    return first, second


(R1, A1, E1), (R2, A2, E2) = filter_constants()


def columns(rows, cols):
    return [(slice(y, y + 8), slice(x, x + 128)) for y in range(0, rows, 8) for x in range(0, cols, 128)]


def peak_kernel(vel, peak):
    planes, rows, cols = vel.shape[1:]
    total = None
    for at in columns(rows, cols):
        for k in range(planes):
            speed = sum(jnp.abs(vel[(comp, k) + at]) for comp in range(3))
            total = speed if total is None else jnp.maximum(total, speed)
    peak[...] = jnp.broadcast_to(jnp.max(total, axis=0, keepdims=True), peak.shape)


def edges_kernel(vel, rightward, leftward):
    planes, rows, cols = vel.shape[1:]
    for at in columns(rows, cols):
        w = [vel[(2, k) + at] for k in range(planes)]
        for comp in range(3):
            u = w if comp == 2 else [vel[(comp, k) + at] for k in range(planes)]
            flux = [a * b for a, b in zip(w, u)]
            for slot, field, root in ((comp, flux, R1), (3 + comp, u, R2)):
                step = [field[k] - field[k - 1] for k in range(1, planes)]
                up, down = step[0], step[-1]
                for k in range(1, planes - 1):
                    up = step[k] + root * up
                    down = step[planes - 2 - k] + root * down
                rightward[(slot,) + at] = up
                leftward[(slot,) + at] = down
            rightward[(6 + comp,) + at] = u[planes - 1]
            leftward[(6 + comp,) + at] = u[0]


def tendency_kernel(vel, from_left, from_right, _, out):
    planes, rows, cols = vel.shape[1:]
    for at in columns(rows, cols):
        w = [vel[(2, k) + at] for k in range(planes)]
        w = [from_left[(8,) + at]] + w + [from_right[(8,) + at]]
        w1 = [A1 * v for v in w]
        for comp in range(3):
            if comp == 2:
                u = w
            else:
                u = [vel[(comp, k) + at] for k in range(planes)]
                u = [from_left[(6 + comp,) + at]] + u + [from_right[(6 + comp,) + at]]
            f1 = [a * b for a, b in zip(w1, u)]
            f2 = [A2 * v for v in u]
            g1 = [f1[k + 1] - f1[k] for k in range(planes + 1)]
            g2 = [f2[k + 1] - f2[k] for k in range(planes + 1)]
            p1 = A1 * from_left[(comp,) + at]
            p2 = A2 * from_left[(3 + comp,) + at]
            forward = []
            for k in range(planes):
                p1 = g1[k] + R1 * p1
                p2 = g2[k] + R2 * p2
                forward.append(p2 - p1)
            q1 = A1 * from_right[(comp,) + at]
            q2 = A2 * from_right[(3 + comp,) + at]
            for k in reversed(range(planes)):
                q1 = g1[k + 1] + R1 * q1
                q2 = g2[k + 1] + R2 * q2
                near = (E1 / A1) * (g1[k] + g1[k + 1]) - (E2 / A2) * (g2[k] - g2[k + 1])
                out[(comp, k) + at] = (forward[k] - (q1 + q2)) + near


def scale_kernel(tendency, peaks, out):
    scale = COURANT / (jnp.max(peaks[...], keepdims=True) + 1e-06)
    out[...] = tendency[...] * jnp.broadcast_to(scale.reshape(1, 1, 1, 1), tendency.shape)


def mesh_groups(shape, free):
    count = 1
    for size in shape:
        count *= size
    groups = {}
    for flat in range(count):
        rest, coords = flat, []
        for size in reversed(shape):
            coords.append(rest % size)
            rest //= size
        coords = coords[::-1]
        key = tuple(c for axis, c in enumerate(coords) if axis not in free)
        groups.setdefault(key, []).append(flat)
    return list(groups.values())


def spread(rows, axes, groups):
    return lax.all_to_all(rows, axes, 0, 0, tiled=True, axis_index_groups=groups)


def work(micros):
    return pl.CostEstimate(flops=int(micros * 1e6), bytes_accessed=int(micros * 3e6), transcendentals=0)


def in_vmem(array):
    return pltpu.with_memory_space_constraint(array, pltpu.VMEM)


def solution(mesh):
    axes = ("gz", "gy")
    slabs, lines = mesh.shape["gz"], mesh.shape["gy"]
    ring = 16
    shape = (slabs // (2 * ring), ring, 2, lines)
    across = mesh_groups(shape, (0, 2, 3))
    along = mesh_groups(shape, (1,))

    def body(velocity):
        _, planes, rows, cols = velocity.shape
        n_across, n_along = len(across[0]), len(along[0])
        local = pl.BlockSpec(memory_space=pltpu.VMEM)
        held = in_vmem(velocity)
        packet = pltpu.VMEM((9, rows, cols), jnp.float32)
        peak = pl.pallas_call(
            peak_kernel,
            out_shape=pltpu.VMEM((n_across, 128), jnp.float32),
            in_specs=[local],
            out_specs=local,
            cost_estimate=work(0.3),
            name="peak",
        )(held)
        rightward, leftward = pl.pallas_call(
            edges_kernel,
            out_shape=(packet, packet),
            in_specs=[local],
            out_specs=(local, local),
            cost_estimate=work(1.0),
            name="edges",
        )(held)
        from_left = in_vmem(lax.ppermute(rightward, "gz", [(i, (i + 1) % slabs) for i in range(slabs)]))
        from_right = in_vmem(lax.ppermute(leftward, "gz", [(i, (i - 1) % slabs) for i in range(slabs)]))
        peak = jnp.max(spread(peak, axes, across), axis=0, keepdims=True)
        peak = jnp.broadcast_to(peak, (n_along, 128))
        peaks = in_vmem(spread(peak, axes, along))
        tendency = pl.pallas_call(
            tendency_kernel,
            out_shape=pltpu.VMEM(velocity.shape, jnp.float32),
            in_specs=[local] * 4,
            out_specs=local,
            cost_estimate=work(1.0),
            name="tendency",
        )(held, from_left, from_right, in_vmem(peak))
        return pl.pallas_call(
            scale_kernel,
            out_shape=jax.ShapeDtypeStruct(velocity.shape, jnp.float32),
            in_specs=[local, local],
            name="scale",
        )(in_vmem(tendency), peaks)

    return jax.shard_map(
        body,
        mesh=mesh,
        in_specs=(P(None, "gz", "gy", None),),
        out_specs=P(None, "gz", "gy", None),
        check_vma=False,
    )
```

```python
import jax
import jax.numpy as jnp
from jax import lax
from jax.experimental import pallas as pl
from jax.experimental.pallas import tpu as pltpu
from jax.sharding import PartitionSpec as P

COURANT = 4.0
FIRST_ROOT = -0.38196601125010515
SECOND_ROOT = -0.18826230851010056
FIRST_OFF, FIRST_NEAR, FIRST_FAR = 1.0 / 3.0, 7.0 / 9.0, 1.0 / 36.0
SECOND_OFF, SECOND_NEAR, SECOND_FAR = 2.0 / 11.0, 12.0 / 11.0, 3.0 / 44.0


def filter_constants():
    r = FIRST_ROOT
    gain = 1.0 / (1.0 + 2.0 * FIRST_OFF * r)
    tail = gain * (FIRST_NEAR * (r - 1.0 / r) + FIRST_FAR * (r * r - 1.0 / (r * r)))
    first = (r, -tail * r / (1.0 - r), -gain * FIRST_FAR * (r - 1.0 / r))
    r = SECOND_ROOT
    gain = 1.0 / (1.0 + 2.0 * SECOND_OFF * r)
    tail = gain * (
        SECOND_NEAR * (r + 1.0 / r)
        + SECOND_FAR * (r * r + 1.0 / (r * r))
        - 2.0 * (SECOND_NEAR + SECOND_FAR)
    )
    second = (r, -tail * r / (1.0 - r), gain * SECOND_FAR * (r - 1.0 / r))
    return first, second


(R1, A1, E1), (R2, A2, E2) = filter_constants()


def columns(rows, cols):
    return [(slice(y, y + 8), slice(x, x + 128)) for y in range(0, rows, 8) for x in range(0, cols, 128)]


def peak_kernel(vel, peak):
    planes, rows, cols = vel.shape[1:]
    total = None
    for at in columns(rows, cols):
        for k in range(planes):
            speed = sum(jnp.abs(vel[(comp, k) + at]) for comp in range(3))
            total = speed if total is None else jnp.maximum(total, speed)
    peak[...] = jnp.broadcast_to(jnp.max(total, axis=0, keepdims=True), peak.shape)


def merge_kernel(peaks, peak):
    peak[...] = jnp.broadcast_to(jnp.max(peaks[...], axis=0, keepdims=True), peak.shape)


def edges_kernel(vel, rightward, leftward):
    planes, rows, cols = vel.shape[1:]
    for at in columns(rows, cols):
        w = [vel[(2, k) + at] for k in range(planes)]
        for comp in range(3):
            u = w if comp == 2 else [vel[(comp, k) + at] for k in range(planes)]
            flux = [a * b for a, b in zip(w, u)]
            for slot, field, root in ((comp, flux, R1), (3 + comp, u, R2)):
                step = [field[k] - field[k - 1] for k in range(1, planes)]
                up, down = step[0], step[-1]
                for k in range(1, planes - 1):
                    up = step[k] + root * up
                    down = step[planes - 2 - k] + root * down
                rightward[(slot,) + at] = up
                leftward[(slot,) + at] = down
            rightward[(6 + comp,) + at] = u[planes - 1]
            leftward[(6 + comp,) + at] = u[0]


def tendency_kernel(vel, from_left, from_right, _, out):
    planes, rows, cols = vel.shape[1:]
    for at in columns(rows, cols):
        w = [vel[(2, k) + at] for k in range(planes)]
        w = [from_left[(8,) + at]] + w + [from_right[(8,) + at]]
        w1 = [A1 * v for v in w]
        for comp in range(3):
            if comp == 2:
                u = w
            else:
                u = [vel[(comp, k) + at] for k in range(planes)]
                u = [from_left[(6 + comp,) + at]] + u + [from_right[(6 + comp,) + at]]
            f1 = [a * b for a, b in zip(w1, u)]
            f2 = [A2 * v for v in u]
            g1 = [f1[k + 1] - f1[k] for k in range(planes + 1)]
            g2 = [f2[k + 1] - f2[k] for k in range(planes + 1)]
            p1 = A1 * from_left[(comp,) + at]
            p2 = A2 * from_left[(3 + comp,) + at]
            forward = []
            for k in range(planes):
                p1 = g1[k] + R1 * p1
                p2 = g2[k] + R2 * p2
                forward.append(p2 - p1)
            q1 = A1 * from_right[(comp,) + at]
            q2 = A2 * from_right[(3 + comp,) + at]
            for k in reversed(range(planes)):
                q1 = g1[k + 1] + R1 * q1
                q2 = g2[k + 1] + R2 * q2
                near = (E1 / A1) * (g1[k] + g1[k + 1]) - (E2 / A2) * (g2[k] - g2[k + 1])
                out[(comp, k) + at] = (forward[k] - (q1 + q2)) + near


def scale_kernel(tendency, peaks, out):
    scale = COURANT / (jnp.max(peaks[...], keepdims=True) + 1e-06)
    out[...] = tendency[...] * jnp.broadcast_to(scale.reshape(1, 1, 1, 1), tendency.shape)


def mesh_groups(shape, free):
    count = 1
    for size in shape:
        count *= size
    groups = {}
    for flat in range(count):
        rest, coords = flat, []
        for size in reversed(shape):
            coords.append(rest % size)
            rest //= size
        coords = coords[::-1]
        key = tuple(c for axis, c in enumerate(coords) if axis not in free)
        groups.setdefault(key, []).append(flat)
    return list(groups.values())


def spread(rows, axes, groups):
    return lax.all_to_all(rows, axes, 0, 0, tiled=True, axis_index_groups=groups)


def work(micros):
    return pl.CostEstimate(flops=int(micros * 1e9), bytes_accessed=int(micros * 3e6), transcendentals=0)


def in_vmem(array):
    return pltpu.with_memory_space_constraint(array, pltpu.VMEM)


def solution(mesh):
    axes = ("gz", "gy")
    slabs, lines = mesh.shape["gz"], mesh.shape["gy"]
    ring = 16
    shape = (slabs // (2 * ring), ring, 2, lines)
    across = mesh_groups(shape, (0, 2, 3))
    along = mesh_groups(shape, (1,))

    def body(velocity):
        _, planes, rows, cols = velocity.shape
        n_across, n_along = len(across[0]), len(along[0])
        local = pl.BlockSpec(memory_space=pltpu.VMEM)
        held = in_vmem(velocity)
        packet = pltpu.VMEM((9, rows, cols), jnp.float32)
        peak = pl.pallas_call(
            peak_kernel,
            out_shape=pltpu.VMEM((n_across, 128), jnp.float32),
            in_specs=[local],
            out_specs=local,
            cost_estimate=work(0.3),
            name="peak",
        )(held)
        rightward, leftward = pl.pallas_call(
            edges_kernel,
            out_shape=(packet, packet),
            in_specs=[local],
            out_specs=(local, local),
            cost_estimate=work(5),
            name="edges",
        )(held)
        from_left = in_vmem(lax.ppermute(rightward, "gz", [(i, (i + 1) % slabs) for i in range(slabs)]))
        from_right = in_vmem(lax.ppermute(leftward, "gz", [(i, (i - 1) % slabs) for i in range(slabs)]))
        merged = pl.pallas_call(
            merge_kernel,
            out_shape=pltpu.VMEM((n_along, 128), jnp.float32),
            in_specs=[local],
            out_specs=local,
            cost_estimate=work(1),
            name="merge",
        )(in_vmem(spread(peak, axes, across)))
        peaks = in_vmem(spread(in_vmem(merged), axes, along))
        tendency = pl.pallas_call(
            tendency_kernel,
            out_shape=pltpu.VMEM(velocity.shape, jnp.float32),
            in_specs=[local] * 4,
            out_specs=local,
            cost_estimate=work(1),
            name="tendency",
        )(held, from_left, from_right, in_vmem(merged))
        return pl.pallas_call(
            scale_kernel,
            out_shape=jax.ShapeDtypeStruct(velocity.shape, jnp.float32),
            in_specs=[local, local],
            name="scale",
        )(in_vmem(tendency), peaks)

    return jax.shard_map(
        body,
        mesh=mesh,
        in_specs=(P(None, "gz", "gy", None),),
        out_specs=P(None, "gz", "gy", None),
        check_vma=False,
    )
```

```python
import jax
import jax.numpy as jnp
from jax import lax
from jax.experimental import pallas as pl
from jax.experimental.pallas import tpu as pltpu
from jax.sharding import PartitionSpec as P

COURANT = 4.0
FIRST_ROOT = -0.38196601125010515
SECOND_ROOT = -0.18826230851010056
FIRST_OFF, FIRST_NEAR, FIRST_FAR = 1.0 / 3.0, 7.0 / 9.0, 1.0 / 36.0
SECOND_OFF, SECOND_NEAR, SECOND_FAR = 2.0 / 11.0, 12.0 / 11.0, 3.0 / 44.0


def filter_constants():
    r = FIRST_ROOT
    gain = 1.0 / (1.0 + 2.0 * FIRST_OFF * r)
    tail = gain * (FIRST_NEAR * (r - 1.0 / r) + FIRST_FAR * (r * r - 1.0 / (r * r)))
    first = (r, -tail * r / (1.0 - r), -gain * FIRST_FAR * (r - 1.0 / r))
    r = SECOND_ROOT
    gain = 1.0 / (1.0 + 2.0 * SECOND_OFF * r)
    tail = gain * (
        SECOND_NEAR * (r + 1.0 / r)
        + SECOND_FAR * (r * r + 1.0 / (r * r))
        - 2.0 * (SECOND_NEAR + SECOND_FAR)
    )
    second = (r, -tail * r / (1.0 - r), gain * SECOND_FAR * (r - 1.0 / r))
    return first, second


(R1, A1, E1), (R2, A2, E2) = filter_constants()


def columns(rows, cols):
    return [(slice(y, y + 8), slice(x, x + 128)) for y in range(0, rows, 8) for x in range(0, cols, 128)]


def peak_kernel(vel, peak, held, sems):
    planes, rows, cols = held.shape[1:]
    count = sems.shape[0]
    share = planes // count
    copies = []
    for part in range(count):
        span = (slice(None), pl.ds(part * share, share))
        copies.append(pltpu.make_async_copy(vel.at[span], held.at[span], sems.at[part]))
        copies[-1].start()
    total = None
    for part in range(count):
        copies[part].wait()
        for k in range(part * share, (part + 1) * share):
            for at in columns(rows, cols):
                speed = sum(jnp.abs(held[(comp, k) + at]) for comp in range(3))
                total = speed if total is None else jnp.maximum(total, speed)
    peak[...] = jnp.broadcast_to(jnp.max(total, axis=0, keepdims=True), peak.shape)


def merge_kernel(peaks, peak):
    peak[...] = jnp.broadcast_to(jnp.max(peaks[...], axis=0, keepdims=True), peak.shape)


def edges_kernel(vel, rightward, leftward):
    planes, rows, cols = vel.shape[1:]
    for at in columns(rows, cols):
        w = [vel[(2, k) + at] for k in range(planes)]
        for comp in range(3):
            u = w if comp == 2 else [vel[(comp, k) + at] for k in range(planes)]
            flux = [a * b for a, b in zip(w, u)]
            for slot, field, root in ((comp, flux, R1), (3 + comp, u, R2)):
                step = [field[k] - field[k - 1] for k in range(1, planes)]
                up, down = step[0], step[-1]
                for k in range(1, planes - 1):
                    up = step[k] + root * up
                    down = step[planes - 2 - k] + root * down
                rightward[(slot,) + at] = up
                leftward[(slot,) + at] = down
            rightward[(6 + comp,) + at] = u[planes - 1]
            leftward[(6 + comp,) + at] = u[0]


def tendency_kernel(vel, from_left, from_right, _, out):
    planes, rows, cols = vel.shape[1:]
    for at in columns(rows, cols):
        w = [vel[(2, k) + at] for k in range(planes)]
        w = [from_left[(8,) + at]] + w + [from_right[(8,) + at]]
        w1 = [A1 * v for v in w]
        for comp in range(3):
            if comp == 2:
                u = w
            else:
                u = [vel[(comp, k) + at] for k in range(planes)]
                u = [from_left[(6 + comp,) + at]] + u + [from_right[(6 + comp,) + at]]
            f1 = [a * b for a, b in zip(w1, u)]
            f2 = [A2 * v for v in u]
            g1 = [f1[k + 1] - f1[k] for k in range(planes + 1)]
            g2 = [f2[k + 1] - f2[k] for k in range(planes + 1)]
            p1 = A1 * from_left[(comp,) + at]
            p2 = A2 * from_left[(3 + comp,) + at]
            forward = []
            for k in range(planes):
                p1 = g1[k] + R1 * p1
                p2 = g2[k] + R2 * p2
                forward.append(p2 - p1)
            q1 = A1 * from_right[(comp,) + at]
            q2 = A2 * from_right[(3 + comp,) + at]
            for k in reversed(range(planes)):
                q1 = g1[k + 1] + R1 * q1
                q2 = g2[k + 1] + R2 * q2
                near = (E1 / A1) * (g1[k] + g1[k + 1]) - (E2 / A2) * (g2[k] - g2[k + 1])
                out[(comp, k) + at] = (forward[k] - (q1 + q2)) + near


def scale_kernel(tendency, peaks, out, staged, sems):
    planes, rows, cols = tendency.shape[1:]
    count = sems.shape[0]
    share = planes // count
    scale = COURANT / (jnp.max(peaks[...], keepdims=True) + 1e-06)
    scale = jnp.broadcast_to(scale, (8, 128))
    copies = []
    for part in range(count):
        for k in range(part * share, (part + 1) * share):
            for comp in range(3):
                for at in columns(rows, cols):
                    staged[(comp, k) + at] = scale * tendency[(comp, k) + at]
        span = (slice(None), pl.ds(part * share, share))
        copies.append(pltpu.make_async_copy(staged.at[span], out.at[span], sems.at[part]))
        copies[-1].start()
    for copy in copies:
        copy.wait()


def mesh_groups(shape, free):
    count = 1
    for size in shape:
        count *= size
    groups = {}
    for flat in range(count):
        rest, coords = flat, []
        for size in reversed(shape):
            coords.append(rest % size)
            rest //= size
        coords = coords[::-1]
        key = tuple(c for axis, c in enumerate(coords) if axis not in free)
        groups.setdefault(key, []).append(flat)
    return list(groups.values())


def spread(rows, axes, groups):
    return lax.all_to_all(rows, axes, 0, 0, tiled=True, axis_index_groups=groups)


def work(micros):
    return pl.CostEstimate(flops=int(micros * 1e9), bytes_accessed=int(micros * 3e6), transcendentals=0)


def in_vmem(array):
    return pltpu.with_memory_space_constraint(array, pltpu.VMEM)


def solution(mesh):
    axes = ("gz", "gy")
    slabs, lines = mesh.shape["gz"], mesh.shape["gy"]
    ring = 16
    shape = (slabs // (2 * ring), ring, 2, lines)
    across = mesh_groups(shape, (0, 2, 3))
    along = mesh_groups(shape, (1,))

    def body(velocity):
        _, planes, rows, cols = velocity.shape
        n_across, n_along = len(across[0]), len(along[0])
        local = pl.BlockSpec(memory_space=pltpu.VMEM)
        packet = pltpu.VMEM((9, rows, cols), jnp.float32)
        peak, held = pl.pallas_call(
            peak_kernel,
            out_shape=(
                pltpu.VMEM((n_along, 128), jnp.float32),
                pltpu.VMEM(velocity.shape, jnp.float32),
            ),
            in_specs=[pl.BlockSpec(memory_space=pl.ANY)],
            out_specs=(local, local),
            scratch_shapes=[pltpu.SemaphoreType.DMA((8,))],
            cost_estimate=work(0.3),
            name="peak",
        )(velocity)
        held = in_vmem(held)
        rightward, leftward = pl.pallas_call(
            edges_kernel,
            out_shape=(packet, packet),
            in_specs=[local],
            out_specs=(local, local),
            cost_estimate=work(1.0),
            name="edges",
        )(held)
        from_left = in_vmem(lax.ppermute(rightward, "gz", [(i, (i + 1) % slabs) for i in range(slabs)]))
        from_right = in_vmem(lax.ppermute(leftward, "gz", [(i, (i - 1) % slabs) for i in range(slabs)]))
        merged = pl.pallas_call(
            merge_kernel,
            out_shape=pltpu.VMEM((n_across, 128), jnp.float32),
            in_specs=[local],
            out_specs=local,
            cost_estimate=work(100.0),
            name="merge",
        )(in_vmem(spread(peak, axes, along)))
        peaks = in_vmem(spread(in_vmem(merged), axes, across))
        tendency = pl.pallas_call(
            tendency_kernel,
            out_shape=pltpu.VMEM(velocity.shape, jnp.float32),
            in_specs=[local] * 4,
            out_specs=local,
            cost_estimate=work(1.0),
            name="tendency",
        )(held, from_left, from_right, in_vmem(merged))
        return pl.pallas_call(
            scale_kernel,
            out_shape=jax.ShapeDtypeStruct(velocity.shape, jnp.float32),
            in_specs=[local, local],
            out_specs=pl.BlockSpec(memory_space=pl.ANY),
            scratch_shapes=[
                pltpu.VMEM(velocity.shape, jnp.float32),
                pltpu.SemaphoreType.DMA((8,)),
            ],
            name="scale",
        )(in_vmem(tendency), peaks)

    return jax.shard_map(
        body,
        mesh=mesh,
        in_specs=(P(None, "gz", "gy", None),),
        out_specs=P(None, "gz", "gy", None),
        check_vma=False,
    )
```

```python
import jax
import jax.numpy as jnp
from jax import lax
from jax.experimental import pallas as pl
from jax.experimental.pallas import tpu as pltpu
from jax.sharding import PartitionSpec as P

COURANT = 4.0
FIRST_ROOT = -0.38196601125010515
SECOND_ROOT = -0.18826230851010056
FIRST_OFF, FIRST_NEAR, FIRST_FAR = 1.0 / 3.0, 7.0 / 9.0, 1.0 / 36.0
SECOND_OFF, SECOND_NEAR, SECOND_FAR = 2.0 / 11.0, 12.0 / 11.0, 3.0 / 44.0


def filter_constants():
    r = FIRST_ROOT
    gain = 1.0 / (1.0 + 2.0 * FIRST_OFF * r)
    tail = gain * (FIRST_NEAR * (r - 1.0 / r) + FIRST_FAR * (r * r - 1.0 / (r * r)))
    first = (r, -tail * r / (1.0 - r), -gain * FIRST_FAR * (r - 1.0 / r))
    r = SECOND_ROOT
    gain = 1.0 / (1.0 + 2.0 * SECOND_OFF * r)
    tail = gain * (
        SECOND_NEAR * (r + 1.0 / r)
        + SECOND_FAR * (r * r + 1.0 / (r * r))
        - 2.0 * (SECOND_NEAR + SECOND_FAR)
    )
    second = (r, -tail * r / (1.0 - r), gain * SECOND_FAR * (r - 1.0 / r))
    return first, second


(R1, A1, E1), (R2, A2, E2) = filter_constants()


def columns(rows, cols):
    return [(slice(y, y + 8), slice(x, x + 128)) for y in range(0, rows, 8) for x in range(0, cols, 128)]


def peak_kernel(vel, peak, held, sems):
    planes, rows, cols = held.shape[1:]
    count = sems.shape[0]
    share = planes // count
    copies = []
    for part in range(count):
        span = (slice(None), pl.ds(part * share, share))
        copies.append(pltpu.make_async_copy(vel.at[span], held.at[span], sems.at[part]))
        copies[-1].start()
    total = None
    for part in range(count):
        copies[part].wait()
        for k in range(part * share, (part + 1) * share):
            for at in columns(rows, cols):
                speed = sum(jnp.abs(held[(comp, k) + at]) for comp in range(3))
                total = speed if total is None else jnp.maximum(total, speed)
    peak[...] = jnp.broadcast_to(jnp.max(total, axis=0, keepdims=True), peak.shape)


def merge_kernel(peaks, peak):
    peak[...] = jnp.broadcast_to(jnp.max(peaks[...], axis=0, keepdims=True), peak.shape)


def edges_kernel(vel, rightward, leftward):
    planes, rows, cols = vel.shape[1:]
    for at in columns(rows, cols):
        w = [vel[(2, k) + at] for k in range(planes)]
        for comp in range(3):
            u = w if comp == 2 else [vel[(comp, k) + at] for k in range(planes)]
            flux = [a * b for a, b in zip(w, u)]
            for slot, field, root in ((comp, flux, R1), (3 + comp, u, R2)):
                step = [field[k] - field[k - 1] for k in range(1, planes)]
                up, down = step[0], step[-1]
                for k in range(1, planes - 1):
                    up = step[k] + root * up
                    down = step[planes - 2 - k] + root * down
                rightward[(slot,) + at] = up
                leftward[(slot,) + at] = down
            rightward[(6 + comp,) + at] = u[planes - 1]
            leftward[(6 + comp,) + at] = u[0]


def step_kernel(peaks, step):
    highest = jnp.max(peaks[...], keepdims=True)
    step[...] = jnp.broadcast_to(COURANT / (highest + 1e-06), step.shape)


def increment_kernel(vel, from_left, from_right, step, out, staged, sems):
    planes, rows, cols = vel.shape[1:]
    gain1 = A1 * step[...]
    gain2 = A2 * step[...]
    copies = []
    for y in range(0, rows, 8):
        for comp in range(3):
            for x in range(0, cols, 128):
                at = (slice(y, y + 8), slice(x, x + 128))
                w = [vel[(2, k) + at] for k in range(planes)]
                w = [from_left[(8,) + at]] + w + [from_right[(8,) + at]]
                u = [vel[(comp, k) + at] for k in range(planes)]
                u = [from_left[(6 + comp,) + at]] + u + [from_right[(6 + comp,) + at]]
                f1 = [gain1 * (a * b) for a, b in zip(w, u)]
                f2 = [gain2 * v for v in u]
                g1 = [f1[k + 1] - f1[k] for k in range(planes + 1)]
                g2 = [f2[k + 1] - f2[k] for k in range(planes + 1)]
                p1 = gain1 * from_left[(comp,) + at]
                p2 = gain2 * from_left[(3 + comp,) + at]
                forward = []
                for k in range(planes):
                    p1 = g1[k] + R1 * p1
                    p2 = g2[k] + R2 * p2
                    forward.append(p2 - p1)
                q1 = gain1 * from_right[(comp,) + at]
                q2 = gain2 * from_right[(3 + comp,) + at]
                for k in reversed(range(planes)):
                    q1 = g1[k + 1] + R1 * q1
                    q2 = g2[k + 1] + R2 * q2
                    near = (E1 / A1) * (g1[k] + g1[k + 1]) - (E2 / A2) * (g2[k] - g2[k + 1])
                    staged[(comp, k) + at] = (forward[k] - (q1 + q2)) + near
            span = (comp, slice(None), pl.ds(y, 8))
            copies.append(pltpu.make_async_copy(staged.at[span], out.at[span], sems.at[len(copies)]))
            copies[-1].start()
    for copy in copies:
        copy.wait()


def mesh_groups(shape, free):
    count = 1
    for size in shape:
        count *= size
    groups = {}
    for flat in range(count):
        rest, coords = flat, []
        for size in reversed(shape):
            coords.append(rest % size)
            rest //= size
        coords = coords[::-1]
        key = tuple(c for axis, c in enumerate(coords) if axis not in free)
        groups.setdefault(key, []).append(flat)
    return list(groups.values())


def spread(rows, axes, groups):
    return lax.all_to_all(rows, axes, 0, 0, tiled=True, axis_index_groups=groups)


def work(micros):
    return pl.CostEstimate(flops=int(micros * 1e9), bytes_accessed=int(micros * 3e6), transcendentals=0)


def in_vmem(array):
    return pltpu.with_memory_space_constraint(array, pltpu.VMEM)


def solution(mesh):
    axes = ("gz", "gy")
    slabs, lines = mesh.shape["gz"], mesh.shape["gy"]
    ring = 16
    shape = (slabs // (2 * ring), ring, 2, lines)
    across = mesh_groups(shape, (0, 3))
    along = mesh_groups(shape, (1, 2))

    def body(velocity):
        _, planes, rows, cols = velocity.shape
        n_across, n_along = len(across[0]), len(along[0])
        local = pl.BlockSpec(memory_space=pltpu.VMEM)
        packet = pltpu.VMEM((9, rows, cols), jnp.float32)
        peak, held = pl.pallas_call(
            peak_kernel,
            out_shape=(
                pltpu.VMEM((n_along, 128), jnp.float32),
                pltpu.VMEM(velocity.shape, jnp.float32),
            ),
            in_specs=[pl.BlockSpec(memory_space=pl.ANY)],
            out_specs=(local, local),
            scratch_shapes=[pltpu.SemaphoreType.DMA((8,))],
            cost_estimate=work(0.3),
            name="peak",
        )(velocity)
        held = in_vmem(held)
        rightward, leftward = pl.pallas_call(
            edges_kernel,
            out_shape=(packet, packet),
            in_specs=[local],
            out_specs=(local, local),
            cost_estimate=work(1.0),
            name="edges",
        )(held)
        from_left = in_vmem(lax.ppermute(rightward, "gz", [(i, (i + 1) % slabs) for i in range(slabs)]))
        from_right = in_vmem(lax.ppermute(leftward, "gz", [(i, (i - 1) % slabs) for i in range(slabs)]))
        merged = pl.pallas_call(
            merge_kernel,
            out_shape=pltpu.VMEM((n_across, 128), jnp.float32),
            in_specs=[local],
            out_specs=local,
            cost_estimate=work(100.0),
            name="merge",
        )(in_vmem(spread(in_vmem(peak), axes, along)))
        merged = in_vmem(merged)
        peaks = in_vmem(spread(merged, axes, across))
        step = pl.pallas_call(
            step_kernel,
            out_shape=pltpu.VMEM((8, 128), jnp.float32),
            in_specs=[local],
            out_specs=local,
            cost_estimate=work(0.1),
            name="step",
        )(peaks)
        return pl.pallas_call(
            increment_kernel,
            out_shape=jax.ShapeDtypeStruct(velocity.shape, jnp.float32),
            in_specs=[local] * 4,
            out_specs=pl.BlockSpec(memory_space=pl.ANY),
            scratch_shapes=[
                pltpu.VMEM(velocity.shape, jnp.float32),
                pltpu.SemaphoreType.DMA((3 * rows // 8,)),
            ],
            name="increment",
        )(held, from_left, from_right, in_vmem(step))

    return jax.shard_map(
        body,
        mesh=mesh,
        in_specs=(P(None, "gz", "gy", None),),
        out_specs=P(None, "gz", "gy", None),
        check_vma=False,
    )
```

```python
import jax
import jax.numpy as jnp
from jax import lax
from jax.experimental import pallas as pl
from jax.experimental.pallas import tpu as pltpu
from jax.sharding import PartitionSpec as P

COURANT = 4.0
FIRST_ROOT = -0.38196601125010515
SECOND_ROOT = -0.18826230851010056
FIRST_OFF, FIRST_NEAR, FIRST_FAR = 1.0 / 3.0, 7.0 / 9.0, 1.0 / 36.0
SECOND_OFF, SECOND_NEAR, SECOND_FAR = 2.0 / 11.0, 12.0 / 11.0, 3.0 / 44.0


def filter_constants():
    r = FIRST_ROOT
    gain = 1.0 / (1.0 + 2.0 * FIRST_OFF * r)
    tail = gain * (FIRST_NEAR * (r - 1.0 / r) + FIRST_FAR * (r * r - 1.0 / (r * r)))
    first = (r, -tail * r / (1.0 - r), -gain * FIRST_FAR * (r - 1.0 / r))
    r = SECOND_ROOT
    gain = 1.0 / (1.0 + 2.0 * SECOND_OFF * r)
    tail = gain * (
        SECOND_NEAR * (r + 1.0 / r)
        + SECOND_FAR * (r * r + 1.0 / (r * r))
        - 2.0 * (SECOND_NEAR + SECOND_FAR)
    )
    second = (r, -tail * r / (1.0 - r), gain * SECOND_FAR * (r - 1.0 / r))
    return first, second


(R1, A1, E1), (R2, A2, E2) = filter_constants()


def columns(rows, cols):
    return [(slice(y, y + 8), slice(x, x + 128)) for y in range(0, rows, 8) for x in range(0, cols, 128)]


def peak_kernel(vel, peak, held, sems):
    planes, rows, cols = held.shape[1:]
    count = sems.shape[0]
    share = planes // count
    copies = []
    for part in range(count):
        span = (slice(None), pl.ds(part * share, share))
        copies.append(pltpu.make_async_copy(vel.at[span], held.at[span], sems.at[part]))
        copies[-1].start()
    total = None
    for part in range(count):
        copies[part].wait()
        for k in range(part * share, (part + 1) * share):
            for at in columns(rows, cols):
                speed = sum(jnp.abs(held[(comp, k) + at]) for comp in range(3))
                total = speed if total is None else jnp.maximum(total, speed)
    peak[...] = jnp.broadcast_to(jnp.max(total, axis=0, keepdims=True), peak.shape)


def merge_kernel(peaks, peak):
    peak[...] = jnp.broadcast_to(jnp.max(peaks[...], axis=0, keepdims=True), peak.shape)


def edges_kernel(vel, rightward, leftward):
    planes, rows, cols = vel.shape[1:]
    for at in columns(rows, cols):
        w = [vel[(2, k) + at] for k in range(planes)]
        for comp in range(3):
            u = w if comp == 2 else [vel[(comp, k) + at] for k in range(planes)]
            flux = [a * b for a, b in zip(w, u)]
            for slot, field, root in ((comp, flux, R1), (3 + comp, u, R2)):
                step = [field[k] - field[k - 1] for k in range(1, planes)]
                up, down = step[0], step[-1]
                for k in range(1, planes - 1):
                    up = step[k] + root * up
                    down = step[planes - 2 - k] + root * down
                rightward[(slot,) + at] = up
                leftward[(slot,) + at] = down
            rightward[(6 + comp,) + at] = u[planes - 1]
            leftward[(6 + comp,) + at] = u[0]


def step_kernel(peaks, step):
    highest = jnp.max(peaks[...], keepdims=True)
    step[...] = jnp.broadcast_to(COURANT / (highest + 1e-06), step.shape)


def increment_kernel(vel, from_left, from_right, step, out, staged, sems):
    planes, rows, cols = vel.shape[1:]
    gain1 = A1 * step[...]
    gain2 = A2 * step[...]
    copies = []
    for y in range(0, rows, 8):
        for comp in range(3):
            for x in range(0, cols, 128):
                at = (slice(y, y + 8), slice(x, x + 128))
                w = [vel[(2, k) + at] for k in range(planes)]
                w = [from_left[(8,) + at]] + w + [from_right[(8,) + at]]
                u = [vel[(comp, k) + at] for k in range(planes)]
                u = [from_left[(6 + comp,) + at]] + u + [from_right[(6 + comp,) + at]]
                f1 = [gain1 * (a * b) for a, b in zip(w, u)]
                f2 = [gain2 * v for v in u]
                g1 = [f1[k + 1] - f1[k] for k in range(planes + 1)]
                g2 = [f2[k + 1] - f2[k] for k in range(planes + 1)]
                p1 = gain1 * from_left[(comp,) + at]
                p2 = gain2 * from_left[(3 + comp,) + at]
                forward = []
                for k in range(planes):
                    p1 = g1[k] + R1 * p1
                    p2 = g2[k] + R2 * p2
                    forward.append(p2 - p1)
                q1 = gain1 * from_right[(comp,) + at]
                q2 = gain2 * from_right[(3 + comp,) + at]
                for k in reversed(range(planes)):
                    q1 = g1[k + 1] + R1 * q1
                    q2 = g2[k + 1] + R2 * q2
                    near = (E1 / A1) * (g1[k] + g1[k + 1]) - (E2 / A2) * (g2[k] - g2[k + 1])
                    staged[(comp, k) + at] = (forward[k] - (q1 + q2)) + near
            span = (comp, slice(None), pl.ds(y, 8))
            copies.append(pltpu.make_async_copy(staged.at[span], out.at[span], sems.at[len(copies)]))
            copies[-1].start()
    for copy in copies:
        copy.wait()


def mesh_groups(shape, free):
    count = 1
    for size in shape:
        count *= size
    groups = {}
    for flat in range(count):
        rest, coords = flat, []
        for size in reversed(shape):
            coords.append(rest % size)
            rest //= size
        coords = coords[::-1]
        key = tuple(c for axis, c in enumerate(coords) if axis not in free)
        groups.setdefault(key, []).append(flat)
    return list(groups.values())


def spread(rows, axes, groups):
    return lax.all_to_all(rows, axes, 0, 0, tiled=True, axis_index_groups=groups)


def work(micros):
    return pl.CostEstimate(flops=int(micros * 1e9), bytes_accessed=int(micros * 3e6), transcendentals=0)


def in_vmem(array):
    return pltpu.with_memory_space_constraint(array, pltpu.VMEM)


def solution(mesh):
    axes = ("gz", "gy")
    slabs, lines = mesh.shape["gz"], mesh.shape["gy"]
    ring = 16
    shape = (slabs // (2 * ring), ring, 2, lines)
    across = [g[::-1] for g in mesh_groups(shape, (0, 3))]
    along = [g[::-1] for g in mesh_groups(shape, (1, 2))]

    def body(velocity):
        _, planes, rows, cols = velocity.shape
        n_across, n_along = len(across[0]), len(along[0])
        local = pl.BlockSpec(memory_space=pltpu.VMEM)
        packet = pltpu.VMEM((9, rows, cols), jnp.float32)
        peak, held = pl.pallas_call(
            peak_kernel,
            out_shape=(
                pltpu.VMEM((n_along, 128), jnp.float32),
                pltpu.VMEM(velocity.shape, jnp.float32),
            ),
            in_specs=[pl.BlockSpec(memory_space=pl.ANY)],
            out_specs=(local, local),
            scratch_shapes=[pltpu.SemaphoreType.DMA((8,))],
            cost_estimate=work(0.3),
            name="peak",
        )(velocity)
        held = in_vmem(held)
        rightward, leftward = pl.pallas_call(
            edges_kernel,
            out_shape=(packet, packet),
            in_specs=[local],
            out_specs=(local, local),
            cost_estimate=work(1.0),
            name="edges",
        )(held)
        from_left = in_vmem(lax.ppermute(rightward, "gz", [(i, (i + 1) % slabs) for i in range(slabs)]))
        from_right = in_vmem(lax.ppermute(leftward, "gz", [(i, (i - 1) % slabs) for i in range(slabs)]))
        merged = pl.pallas_call(
            merge_kernel,
            out_shape=pltpu.VMEM((n_across, 128), jnp.float32),
            in_specs=[local],
            out_specs=local,
            cost_estimate=work(100.0),
            name="merge",
        )(in_vmem(spread(in_vmem(peak), axes, along)))
        merged = in_vmem(merged)
        peaks = in_vmem(spread(merged, axes, across))
        step = pl.pallas_call(
            step_kernel,
            out_shape=pltpu.VMEM((8, 128), jnp.float32),
            in_specs=[local],
            out_specs=local,
            cost_estimate=work(0.1),
            name="step",
        )(peaks)
        return pl.pallas_call(
            increment_kernel,
            out_shape=jax.ShapeDtypeStruct(velocity.shape, jnp.float32),
            in_specs=[local] * 4,
            out_specs=pl.BlockSpec(memory_space=pl.ANY),
            scratch_shapes=[
                pltpu.VMEM(velocity.shape, jnp.float32),
                pltpu.SemaphoreType.DMA((3 * rows // 8,)),
            ],
            name="increment",
        )(held, from_left, from_right, in_vmem(step))

    return jax.shard_map(
        body,
        mesh=mesh,
        in_specs=(P(None, "gz", "gy", None),),
        out_specs=P(None, "gz", "gy", None),
        check_vma=False,
    )
```

```python
import jax
import jax.numpy as jnp
from jax import lax
from jax.experimental import pallas as pl
from jax.experimental.pallas import tpu as pltpu
from jax.sharding import PartitionSpec as P

COURANT = 4.0
FIRST_ROOT = -0.38196601125010515
SECOND_ROOT = -0.18826230851010056
FIRST_OFF, FIRST_NEAR, FIRST_FAR = 1.0 / 3.0, 7.0 / 9.0, 1.0 / 36.0
SECOND_OFF, SECOND_NEAR, SECOND_FAR = 2.0 / 11.0, 12.0 / 11.0, 3.0 / 44.0


def filter_constants():
    r = FIRST_ROOT
    gain = 1.0 / (1.0 + 2.0 * FIRST_OFF * r)
    tail = gain * (FIRST_NEAR * (r - 1.0 / r) + FIRST_FAR * (r * r - 1.0 / (r * r)))
    first = (r, -tail * r / (1.0 - r), -gain * FIRST_FAR * (r - 1.0 / r))
    r = SECOND_ROOT
    gain = 1.0 / (1.0 + 2.0 * SECOND_OFF * r)
    tail = gain * (
        SECOND_NEAR * (r + 1.0 / r)
        + SECOND_FAR * (r * r + 1.0 / (r * r))
        - 2.0 * (SECOND_NEAR + SECOND_FAR)
    )
    second = (r, -tail * r / (1.0 - r), gain * SECOND_FAR * (r - 1.0 / r))
    return first, second


(R1, A1, E1), (R2, A2, E2) = filter_constants()


def columns(rows, cols):
    return [(slice(y, y + 8), slice(x, x + 128)) for y in range(0, rows, 8) for x in range(0, cols, 128)]


def peak_kernel(vel, peak, held, sems):
    planes, rows, cols = held.shape[1:]
    count = sems.shape[0]
    share = planes // count
    copies = []
    for part in range(count):
        span = (slice(None), pl.ds(part * share, share))
        copies.append(pltpu.make_async_copy(vel.at[span], held.at[span], sems.at[part]))
        copies[-1].start()
    total = None
    for part in range(count):
        copies[part].wait()
        for k in range(part * share, (part + 1) * share):
            for at in columns(rows, cols):
                speed = sum(jnp.abs(held[(comp, k) + at]) for comp in range(3))
                total = speed if total is None else jnp.maximum(total, speed)
    peak[...] = jnp.broadcast_to(jnp.max(total, axis=0, keepdims=True), peak.shape)


def merge_kernel(peaks, peak):
    peak[...] = jnp.broadcast_to(jnp.max(peaks[...], axis=0, keepdims=True), peak.shape)


def edges_kernel(vel, rightward, leftward):
    planes, rows, cols = vel.shape[1:]
    for at in columns(rows, cols):
        w = [vel[(2, k) + at] for k in range(planes)]
        for comp in range(3):
            u = w if comp == 2 else [vel[(comp, k) + at] for k in range(planes)]
            flux = [a * b for a, b in zip(w, u)]
            for slot, field, root in ((comp, flux, R1), (3 + comp, u, R2)):
                step = [field[k] - field[k - 1] for k in range(1, planes)]
                up, down = step[0], step[-1]
                for k in range(1, planes - 1):
                    up = step[k] + root * up
                    down = step[planes - 2 - k] + root * down
                rightward[(slot,) + at] = up
                leftward[(slot,) + at] = down
            rightward[(6 + comp,) + at] = u[planes - 1]
            leftward[(6 + comp,) + at] = u[0]


def step_kernel(peaks, step):
    highest = jnp.max(peaks[...], keepdims=True)
    step[...] = jnp.broadcast_to(COURANT / (highest + 1e-06), step.shape)


def increment_kernel(vel, from_left, from_right, step, out, staged, sems):
    planes, rows, cols = vel.shape[1:]
    gain1 = A1 * step[...]
    gain2 = A2 * step[...]
    copies = []
    for y in range(0, rows, 8):
        for comp in range(3):
            for x in range(0, cols, 128):
                at = (slice(y, y + 8), slice(x, x + 128))
                w = [vel[(2, k) + at] for k in range(planes)]
                w = [from_left[(8,) + at]] + w + [from_right[(8,) + at]]
                u = [vel[(comp, k) + at] for k in range(planes)]
                u = [from_left[(6 + comp,) + at]] + u + [from_right[(6 + comp,) + at]]
                f1 = [gain1 * (a * b) for a, b in zip(w, u)]
                f2 = [gain2 * v for v in u]
                g1 = [f1[k + 1] - f1[k] for k in range(planes + 1)]
                g2 = [f2[k + 1] - f2[k] for k in range(planes + 1)]
                p1 = gain1 * from_left[(comp,) + at]
                p2 = gain2 * from_left[(3 + comp,) + at]
                forward = []
                for k in range(planes):
                    p1 = g1[k] + R1 * p1
                    p2 = g2[k] + R2 * p2
                    forward.append(p2 - p1)
                q1 = gain1 * from_right[(comp,) + at]
                q2 = gain2 * from_right[(3 + comp,) + at]
                for k in reversed(range(planes)):
                    q1 = g1[k + 1] + R1 * q1
                    q2 = g2[k + 1] + R2 * q2
                    near = (E1 / A1) * (g1[k] + g1[k + 1]) - (E2 / A2) * (g2[k] - g2[k + 1])
                    staged[(comp, k) + at] = (forward[k] - (q1 + q2)) + near
            span = (comp, slice(None), pl.ds(y, 8))
            copies.append(pltpu.make_async_copy(staged.at[span], out.at[span], sems.at[len(copies)]))
            copies[-1].start()
    for copy in copies:
        copy.wait()


def mesh_groups(shape, free):
    count = 1
    for size in shape:
        count *= size
    groups = {}
    for flat in range(count):
        rest, coords = flat, []
        for size in reversed(shape):
            coords.append(rest % size)
            rest //= size
        coords = coords[::-1]
        key = tuple(c for axis, c in enumerate(coords) if axis not in free)
        groups.setdefault(key, []).append(flat)
    return list(groups.values())


def far_first(group, columns, lines):
    def distance(place):
        x, y = divmod(place, lines)
        return min(x, columns - x) + min(y, lines - y)

    places = sorted(range(len(group)), key=lambda place: (distance(place), place), reverse=True)
    return [group[place] for place in places]


def spread(rows, axes, groups):
    return lax.all_to_all(rows, axes, 0, 0, tiled=True, axis_index_groups=groups)


def work(micros):
    return pl.CostEstimate(flops=int(micros * 1e9), bytes_accessed=int(micros * 3e6), transcendentals=0)


def in_vmem(array):
    return pltpu.with_memory_space_constraint(array, pltpu.VMEM)


def solution(mesh):
    axes = ("gz", "gy")
    slabs, lines = mesh.shape["gz"], mesh.shape["gy"]
    ring = 16
    shape = (slabs // (2 * ring), ring, 2, lines)
    along = [group[::-1] for group in mesh_groups(shape, (1, 2))]
    across = [far_first(group, shape[0], lines) for group in mesh_groups(shape, (0, 3))]

    def body(velocity):
        _, planes, rows, cols = velocity.shape
        n_across, n_along = len(across[0]), len(along[0])
        local = pl.BlockSpec(memory_space=pltpu.VMEM)
        packet = pltpu.VMEM((9, rows, cols), jnp.float32)
        peak, held = pl.pallas_call(
            peak_kernel,
            out_shape=(
                pltpu.VMEM((n_along, 128), jnp.float32),
                pltpu.VMEM(velocity.shape, jnp.float32),
            ),
            in_specs=[pl.BlockSpec(memory_space=pl.ANY)],
            out_specs=(local, local),
            scratch_shapes=[pltpu.SemaphoreType.DMA((8,))],
            cost_estimate=work(0.3),
            name="peak",
        )(velocity)
        held = in_vmem(held)
        rightward, leftward = pl.pallas_call(
            edges_kernel,
            out_shape=(packet, packet),
            in_specs=[local],
            out_specs=(local, local),
            cost_estimate=work(1.0),
            name="edges",
        )(held)
        from_left = in_vmem(lax.ppermute(rightward, "gz", [(i, (i + 1) % slabs) for i in range(slabs)]))
        from_right = in_vmem(lax.ppermute(leftward, "gz", [(i, (i - 1) % slabs) for i in range(slabs)]))
        merged = pl.pallas_call(
            merge_kernel,
            out_shape=pltpu.VMEM((n_across, 128), jnp.float32),
            in_specs=[local],
            out_specs=local,
            cost_estimate=work(100.0),
            name="merge",
        )(in_vmem(spread(in_vmem(peak), axes, along)))
        merged = in_vmem(merged)
        peaks = in_vmem(spread(merged, axes, across))
        step = pl.pallas_call(
            step_kernel,
            out_shape=pltpu.VMEM((8, 128), jnp.float32),
            in_specs=[local],
            out_specs=local,
            cost_estimate=work(0.1),
            name="step",
        )(peaks)
        return pl.pallas_call(
            increment_kernel,
            out_shape=jax.ShapeDtypeStruct(velocity.shape, jnp.float32),
            in_specs=[local] * 4,
            out_specs=pl.BlockSpec(memory_space=pl.ANY),
            scratch_shapes=[
                pltpu.VMEM(velocity.shape, jnp.float32),
                pltpu.SemaphoreType.DMA((3 * rows // 8,)),
            ],
            name="increment",
        )(held, from_left, from_right, in_vmem(step))

    return jax.shard_map(
        body,
        mesh=mesh,
        in_specs=(P(None, "gz", "gy", None),),
        out_specs=P(None, "gz", "gy", None),
        check_vma=False,
    )
```

```python
import jax
import jax.numpy as jnp
from jax import lax
from jax.experimental import pallas as pl
from jax.experimental.pallas import tpu as pltpu
from jax.sharding import PartitionSpec as P

COURANT = 4.0
FIRST_ROOT = -0.38196601125010515
SECOND_ROOT = -0.18826230851010056
FIRST_OFF, FIRST_NEAR, FIRST_FAR = 1.0 / 3.0, 7.0 / 9.0, 1.0 / 36.0
SECOND_OFF, SECOND_NEAR, SECOND_FAR = 2.0 / 11.0, 12.0 / 11.0, 3.0 / 44.0


def filter_constants():
    r = FIRST_ROOT
    gain = 1.0 / (1.0 + 2.0 * FIRST_OFF * r)
    tail = gain * (FIRST_NEAR * (r - 1.0 / r) + FIRST_FAR * (r * r - 1.0 / (r * r)))
    first = (r, -tail * r / (1.0 - r), -gain * FIRST_FAR * (r - 1.0 / r))
    r = SECOND_ROOT
    gain = 1.0 / (1.0 + 2.0 * SECOND_OFF * r)
    tail = gain * (
        SECOND_NEAR * (r + 1.0 / r)
        + SECOND_FAR * (r * r + 1.0 / (r * r))
        - 2.0 * (SECOND_NEAR + SECOND_FAR)
    )
    second = (r, -tail * r / (1.0 - r), gain * SECOND_FAR * (r - 1.0 / r))
    return first, second


(R1, A1, E1), (R2, A2, E2) = filter_constants()


def columns(rows, cols):
    return [(slice(y, y + 8), slice(x, x + 128)) for y in range(0, rows, 8) for x in range(0, cols, 128)]


def peak_kernel(vel, peak, held, sems):
    planes, rows, cols = held.shape[1:]
    count = sems.shape[0]
    share = planes // count
    copies = []
    for part in range(count):
        span = (slice(None), pl.ds(part * share, share))
        copies.append(pltpu.make_async_copy(vel.at[span], held.at[span], sems.at[part]))
        copies[-1].start()
    total = None
    for part in range(count):
        copies[part].wait()
        for k in range(part * share, (part + 1) * share):
            for at in columns(rows, cols):
                speed = sum(jnp.abs(held[(comp, k) + at]) for comp in range(3))
                total = speed if total is None else jnp.maximum(total, speed)
    peak[...] = jnp.broadcast_to(jnp.max(total, axis=0, keepdims=True), peak.shape)


def merge_kernel(peaks, peak):
    peak[...] = jnp.broadcast_to(jnp.max(peaks[...], axis=0, keepdims=True), peak.shape)


def edges_kernel(vel, rightward, leftward):
    planes, rows, cols = vel.shape[1:]
    for at in columns(rows, cols):
        w = [vel[(2, k) + at] for k in range(planes)]
        for comp in range(3):
            u = w if comp == 2 else [vel[(comp, k) + at] for k in range(planes)]
            flux = [a * b for a, b in zip(w, u)]
            for slot, field, root in ((comp, flux, R1), (3 + comp, u, R2)):
                step = [field[k] - field[k - 1] for k in range(1, planes)]
                up, down = step[0], step[-1]
                for k in range(1, planes - 1):
                    up = step[k] + root * up
                    down = step[planes - 2 - k] + root * down
                rightward[(slot,) + at] = up
                leftward[(slot,) + at] = down
            rightward[(6 + comp,) + at] = u[planes - 1]
            leftward[(6 + comp,) + at] = u[0]


def increment_kernel(vel, from_left, from_right, peaks, out, staged, sems):
    planes, rows, cols = vel.shape[1:]
    step = jnp.broadcast_to(COURANT / (jnp.max(peaks[...], keepdims=True) + 1e-06), (8, 128))
    gain1 = A1 * step
    gain2 = A2 * step
    copies = []
    for y in range(0, rows, 8):
        for comp in range(3):
            for x in range(0, cols, 128):
                at = (slice(y, y + 8), slice(x, x + 128))
                w = [vel[(2, k) + at] for k in range(planes)]
                w = [from_left[(8,) + at]] + w + [from_right[(8,) + at]]
                u = [vel[(comp, k) + at] for k in range(planes)]
                u = [from_left[(6 + comp,) + at]] + u + [from_right[(6 + comp,) + at]]
                f1 = [gain1 * (a * b) for a, b in zip(w, u)]
                f2 = [gain2 * v for v in u]
                g1 = [f1[k + 1] - f1[k] for k in range(planes + 1)]
                g2 = [f2[k + 1] - f2[k] for k in range(planes + 1)]
                p1 = gain1 * from_left[(comp,) + at]
                p2 = gain2 * from_left[(3 + comp,) + at]
                forward = []
                for k in range(planes):
                    p1 = g1[k] + R1 * p1
                    p2 = g2[k] + R2 * p2
                    forward.append(p2 - p1)
                q1 = gain1 * from_right[(comp,) + at]
                q2 = gain2 * from_right[(3 + comp,) + at]
                for k in reversed(range(planes)):
                    q1 = g1[k + 1] + R1 * q1
                    q2 = g2[k + 1] + R2 * q2
                    near = (E1 / A1) * (g1[k] + g1[k + 1]) - (E2 / A2) * (g2[k] - g2[k + 1])
                    staged[(comp, k) + at] = (forward[k] - (q1 + q2)) + near
            span = (comp, slice(None), pl.ds(y, 8))
            copies.append(pltpu.make_async_copy(staged.at[span], out.at[span], sems.at[len(copies)]))
            copies[-1].start()
    for copy in copies:
        copy.wait()


def mesh_groups(shape, free):
    count = 1
    for size in shape:
        count *= size
    groups = {}
    for flat in range(count):
        rest, coords = flat, []
        for size in reversed(shape):
            coords.append(rest % size)
            rest //= size
        coords = coords[::-1]
        key = tuple(c for axis, c in enumerate(coords) if axis not in free)
        groups.setdefault(key, []).append(flat)
    return list(groups.values())


def far_first(group, columns, lines):
    def distance(place):
        x, y = divmod(place, lines)
        return min(x, columns - x) + min(y, lines - y)

    places = sorted(range(len(group)), key=lambda place: (distance(place), place), reverse=True)
    return [group[place] for place in places]


def spread(rows, axes, groups):
    return lax.all_to_all(rows, axes, 0, 0, tiled=True, axis_index_groups=groups)


def work(micros):
    return pl.CostEstimate(flops=int(micros * 1e9), bytes_accessed=int(micros * 3e6), transcendentals=0)


def in_vmem(array):
    return pltpu.with_memory_space_constraint(array, pltpu.VMEM)


def solution(mesh):
    axes = ("gz", "gy")
    slabs, lines = mesh.shape["gz"], mesh.shape["gy"]
    ring = 16
    shape = (slabs // (2 * ring), ring, 2, lines)
    along = [group[::-1] for group in mesh_groups(shape, (1, 2))]
    across = [far_first(group, shape[0], lines) for group in mesh_groups(shape, (0, 3))]

    def body(velocity):
        _, planes, rows, cols = velocity.shape
        n_across, n_along = len(across[0]), len(along[0])
        local = pl.BlockSpec(memory_space=pltpu.VMEM)
        packet = pltpu.VMEM((9, rows, cols), jnp.float32)
        peak, held = pl.pallas_call(
            peak_kernel,
            out_shape=(
                pltpu.VMEM((n_along, 128), jnp.float32),
                pltpu.VMEM(velocity.shape, jnp.float32),
            ),
            in_specs=[pl.BlockSpec(memory_space=pl.ANY)],
            out_specs=(local, local),
            scratch_shapes=[pltpu.SemaphoreType.DMA((8,))],
            cost_estimate=work(0.3),
            name="peak",
        )(velocity)
        held = in_vmem(held)
        rightward, leftward = pl.pallas_call(
            edges_kernel,
            out_shape=(packet, packet),
            in_specs=[local],
            out_specs=(local, local),
            cost_estimate=work(1.0),
            name="edges",
        )(held)
        from_left = in_vmem(lax.ppermute(rightward, "gz", [(i, (i + 1) % slabs) for i in range(slabs)]))
        from_right = in_vmem(lax.ppermute(leftward, "gz", [(i, (i - 1) % slabs) for i in range(slabs)]))
        merged = pl.pallas_call(
            merge_kernel,
            out_shape=pltpu.VMEM((n_across, 128), jnp.float32),
            in_specs=[local],
            out_specs=local,
            cost_estimate=work(100.0),
            name="merge",
        )(in_vmem(spread(in_vmem(peak), axes, along)))
        merged = in_vmem(merged)
        peaks = in_vmem(spread(merged, axes, across))
        return pl.pallas_call(
            increment_kernel,
            out_shape=jax.ShapeDtypeStruct(velocity.shape, jnp.float32),
            in_specs=[local] * 4,
            out_specs=pl.BlockSpec(memory_space=pl.ANY),
            scratch_shapes=[
                pltpu.VMEM(velocity.shape, jnp.float32),
                pltpu.SemaphoreType.DMA((3 * rows // 8,)),
            ],
            name="increment",
        )(held, from_left, from_right, peaks)

    return jax.shard_map(
        body,
        mesh=mesh,
        in_specs=(P(None, "gz", "gy", None),),
        out_specs=P(None, "gz", "gy", None),
        check_vma=False,
    )
```

```python
import jax
import jax.numpy as jnp
from jax import lax
from jax.experimental import pallas as pl
from jax.experimental.pallas import tpu as pltpu
from jax.sharding import PartitionSpec as P

COURANT = 4.0
FIRST_ROOT = -0.38196601125010515
SECOND_ROOT = -0.18826230851010056
FIRST_OFF, FIRST_NEAR, FIRST_FAR = 1.0 / 3.0, 7.0 / 9.0, 1.0 / 36.0
SECOND_OFF, SECOND_NEAR, SECOND_FAR = 2.0 / 11.0, 12.0 / 11.0, 3.0 / 44.0


def filter_constants():
    r = FIRST_ROOT
    gain = 1.0 / (1.0 + 2.0 * FIRST_OFF * r)
    tail = gain * (FIRST_NEAR * (r - 1.0 / r) + FIRST_FAR * (r * r - 1.0 / (r * r)))
    first = (r, -tail * r / (1.0 - r), -gain * FIRST_FAR * (r - 1.0 / r))
    r = SECOND_ROOT
    gain = 1.0 / (1.0 + 2.0 * SECOND_OFF * r)
    tail = gain * (
        SECOND_NEAR * (r + 1.0 / r)
        + SECOND_FAR * (r * r + 1.0 / (r * r))
        - 2.0 * (SECOND_NEAR + SECOND_FAR)
    )
    second = (r, -tail * r / (1.0 - r), gain * SECOND_FAR * (r - 1.0 / r))
    return first, second


(R1, A1, E1), (R2, A2, E2) = filter_constants()


def columns(rows, cols):
    return [(slice(y, y + 8), slice(x, x + 128)) for y in range(0, rows, 8) for x in range(0, cols, 128)]


def peak_kernel(vel, peak, held, sems):
    planes, rows, cols = held.shape[1:]
    copy = pltpu.make_async_copy(vel, held, sems.at[0])
    copy.start()
    copy.wait()
    totals = [None] * 8
    for k in range(planes):
        for i, at in enumerate(columns(rows, cols)):
            slot = (k * len(columns(rows, cols)) + i) % len(totals)
            speed = sum(jnp.abs(held[(comp, k) + at]) for comp in range(3))
            totals[slot] = speed if totals[slot] is None else jnp.maximum(totals[slot], speed)
    while len(totals) > 1:
        totals = [jnp.maximum(a, b) for a, b in zip(totals[::2], totals[1::2])]
    total = totals[0]
    peak[...] = jnp.broadcast_to(jnp.max(total, axis=0, keepdims=True), peak.shape)


def merge_kernel(peaks, peak):
    peak[...] = jnp.broadcast_to(jnp.max(peaks[...], axis=0, keepdims=True), peak.shape)


def edges_kernel(vel, rightward, leftward):
    planes, rows, cols = vel.shape[1:]
    for at in columns(rows, cols):
        w = [vel[(2, k) + at] for k in range(planes)]
        for comp in range(3):
            u = w if comp == 2 else [vel[(comp, k) + at] for k in range(planes)]
            flux = [a * b for a, b in zip(w, u)]
            for slot, field, root in ((comp, flux, R1), (3 + comp, u, R2)):
                step = [field[k] - field[k - 1] for k in range(1, planes)]
                up, down = step[0], step[-1]
                for k in range(1, planes - 1):
                    up = step[k] + root * up
                    down = step[planes - 2 - k] + root * down
                rightward[(slot,) + at] = up
                leftward[(slot,) + at] = down
            rightward[(6 + comp,) + at] = u[planes - 1]
            leftward[(6 + comp,) + at] = u[0]


def increment_kernel(vel, from_left, from_right, peaks, out, staged, sems):
    planes, rows, cols = vel.shape[1:]
    step = jnp.broadcast_to(COURANT / (jnp.max(peaks[...], keepdims=True) + 1e-06), (8, 128))
    gain1 = A1 * step
    gain2 = A2 * step
    copies = []
    for y in range(0, rows, 8):
        for comp in range(3):
            for x in range(0, cols, 128):
                at = (slice(y, y + 8), slice(x, x + 128))
                w = [vel[(2, k) + at] for k in range(planes)]
                w = [from_left[(8,) + at]] + w + [from_right[(8,) + at]]
                u = [vel[(comp, k) + at] for k in range(planes)]
                u = [from_left[(6 + comp,) + at]] + u + [from_right[(6 + comp,) + at]]
                f1 = [gain1 * (a * b) for a, b in zip(w, u)]
                f2 = [gain2 * v for v in u]
                g1 = [f1[k + 1] - f1[k] for k in range(planes + 1)]
                g2 = [f2[k + 1] - f2[k] for k in range(planes + 1)]
                p1 = gain1 * from_left[(comp,) + at]
                p2 = gain2 * from_left[(3 + comp,) + at]
                forward = []
                for k in range(planes):
                    p1 = g1[k] + R1 * p1
                    p2 = g2[k] + R2 * p2
                    forward.append(p2 - p1)
                q1 = gain1 * from_right[(comp,) + at]
                q2 = gain2 * from_right[(3 + comp,) + at]
                for k in reversed(range(planes)):
                    q1 = g1[k + 1] + R1 * q1
                    q2 = g2[k + 1] + R2 * q2
                    near = (E1 / A1) * (g1[k] + g1[k + 1]) - (E2 / A2) * (g2[k] - g2[k + 1])
                    staged[(comp, k) + at] = (forward[k] - (q1 + q2)) + near
            span = (comp, slice(None), pl.ds(y, 8))
            copies.append(pltpu.make_async_copy(staged.at[span], out.at[span], sems.at[len(copies)]))
            copies[-1].start()
    for copy in copies:
        copy.wait()


def mesh_groups(shape, free):
    count = 1
    for size in shape:
        count *= size
    groups = {}
    for flat in range(count):
        rest, coords = flat, []
        for size in reversed(shape):
            coords.append(rest % size)
            rest //= size
        coords = coords[::-1]
        key = tuple(c for axis, c in enumerate(coords) if axis not in free)
        groups.setdefault(key, []).append(flat)
    return list(groups.values())


def far_first(group, columns, lines):
    def distance(place):
        x, y = divmod(place, lines)
        return min(x, columns - x) + min(y, lines - y)

    places = sorted(range(len(group)), key=lambda place: (distance(place), place), reverse=True)
    return [group[place] for place in places]


def spread(rows, axes, groups):
    return lax.all_to_all(rows, axes, 0, 0, tiled=True, axis_index_groups=groups)


def work(micros):
    return pl.CostEstimate(flops=int(micros * 1e9), bytes_accessed=int(micros * 3e6), transcendentals=0)


def in_vmem(array):
    return pltpu.with_memory_space_constraint(array, pltpu.VMEM)


def solution(mesh):
    axes = ("gz", "gy")
    slabs, lines = mesh.shape["gz"], mesh.shape["gy"]
    ring = 16
    shape = (slabs // (2 * ring), ring, 2, lines)
    along = [group[::-1] for group in mesh_groups(shape, (1, 2))]
    across = [far_first(group, shape[0], lines) for group in mesh_groups(shape, (0, 3))]

    def body(velocity):
        _, planes, rows, cols = velocity.shape
        n_across, n_along = len(across[0]), len(along[0])
        local = pl.BlockSpec(memory_space=pltpu.VMEM)
        packet = pltpu.VMEM((9, rows, cols), jnp.float32)
        peak, held = pl.pallas_call(
            peak_kernel,
            out_shape=(
                pltpu.VMEM((n_along, 128), jnp.float32),
                pltpu.VMEM(velocity.shape, jnp.float32),
            ),
            in_specs=[pl.BlockSpec(memory_space=pl.ANY)],
            out_specs=(local, local),
            scratch_shapes=[pltpu.SemaphoreType.DMA((1,))],
            cost_estimate=work(0.3),
            name="peak",
        )(velocity)
        held = in_vmem(held)
        rightward, leftward = pl.pallas_call(
            edges_kernel,
            out_shape=(packet, packet),
            in_specs=[local],
            out_specs=(local, local),
            cost_estimate=work(1.0),
            name="edges",
        )(held)
        from_left = in_vmem(lax.ppermute(rightward, "gz", [(i, (i + 1) % slabs) for i in range(slabs)]))
        from_right = in_vmem(lax.ppermute(leftward, "gz", [(i, (i - 1) % slabs) for i in range(slabs)]))
        merged = pl.pallas_call(
            merge_kernel,
            out_shape=pltpu.VMEM((n_across, 128), jnp.float32),
            in_specs=[local],
            out_specs=local,
            cost_estimate=work(100.0),
            name="merge",
        )(in_vmem(spread(in_vmem(peak), axes, along)))
        merged = in_vmem(merged)
        peaks = in_vmem(spread(merged, axes, across))
        return pl.pallas_call(
            increment_kernel,
            out_shape=jax.ShapeDtypeStruct(velocity.shape, jnp.float32),
            in_specs=[local] * 4,
            out_specs=pl.BlockSpec(memory_space=pl.ANY),
            scratch_shapes=[
                pltpu.VMEM(velocity.shape, jnp.float32),
                pltpu.SemaphoreType.DMA((3 * rows // 8,)),
            ],
            name="increment",
        )(held, from_left, from_right, peaks)

    return jax.shard_map(
        body,
        mesh=mesh,
        in_specs=(P(None, "gz", "gy", None),),
        out_specs=P(None, "gz", "gy", None),
        check_vma=False,
    )
```
